256 devices in a mesh: head: 8 (over x, z_lo), blk: 32 (over y, z_hi, core).
Axes of the slice: x: 4, y: 4, z: 8 (z_hi: 4, z_lo: 2; z = z_hi * 2 + z_lo), core: 2. Of those that a mesh axis runs over, the one named last changes fastest.
Arguments:
- queries: bfloat16 [8192, 3072], P(('blk', 'head')), may hold values from -6 to 6
- key_rows: bfloat16 [8192, 3072], P(('blk', 'head')), may hold values from -6 to 6
- values: bfloat16 [8192, 3072], P(('blk', 'head')), may hold values from -4 to 4
- tile_mask: int32 [64, 64], replicated, may hold values from 0 to 1, as said below
Outputs:
- attended: float32 [8192, 3072], P(('blk', 'head'))
The draws below stay inside these ranges and needn't reach their ends.
Inputs may be any that keep to these rules, and one draw needn't show every extreme that they name: tile_mask[i, j] is 1 exactly when key tile j lies within query tile i's 3-D window; tile i sits at time level i // 16, row (i // 4) % 4 and column i % 4 of a grid of 4 x 4 x 4 tiles; each time level of query tiles has its own window, whose backward and forward half-widths along each of the three directions are 1 or 2 tiles, drawn separately.
All inputs are finite; a program needn't handle non-finite values.
Results may differ from the reference program's by a relative error of at most 0.0025.
Values may be sent and summed in bfloat16 or wider, within the bound.
A program may use at most 128 MiB of HBM per device.

```python
import jax
import jax.numpy as jnp
from jax import lax

HEADS = 24
HEAD_DIM = 128
HD = 3072
TILE = 128
TH = 4
TW = 4
SLAB = 256
SLABS = 32
TOKENS = 8192
TILES = 64
TT = 4


def draw_queries(key, part):
    key = jax.random.fold_in(key, 1)
    drawn = jnp.clip(jax.random.normal(key, (TOKENS, HD), jnp.float32), -6.0, 6.0)
    return drawn.astype(jnp.bfloat16)


def draw_key_rows(key, part):
    key = jax.random.fold_in(key, 2)
    drawn = jnp.clip(jax.random.normal(key, (TOKENS, HD), jnp.float32), -6.0, 6.0)
    return drawn.astype(jnp.bfloat16)


def draw_tile_mask(key, part):
    key = jax.random.fold_in(key, 3)
    widths = jax.random.randint(key, (TT, 6), 1, 3)
    tile_index = jnp.arange(TILES)
    tile_level = tile_index // (TH * TW)
    tile_row = tile_index // TW % TH
    tile_column = tile_index % TW
    own = widths[tile_level]
    level_step = tile_level[None, :] - tile_level[:, None]
    row_step = tile_row[None, :] - tile_row[:, None]
    column_step = tile_column[None, :] - tile_column[:, None]
    near_level = (level_step >= -own[:, 0:1]) & (level_step <= own[:, 1:2])
    near_row = (row_step >= -own[:, 2:3]) & (row_step <= own[:, 3:4])
    near_column = (column_step >= -own[:, 4:5]) & (column_step <= own[:, 5:6])
    return (near_level & near_row & near_column).astype(jnp.int32)


def block_levels(rng, extent, shards, low, high):
    def one(dim, shards_of):
        steps = jax.random.uniform(jax.random.fold_in(jax.random.fold_in(rng, 6), dim), (shards_of,), jnp.float32, low / len(shards), high / len(shards))
        return jnp.repeat(jnp.exp(steps), extent[dim] // shards_of).reshape((-1,) + (1,) * (len(extent) - dim - 1))

    loudness = one(*shards[0])
    for cut in shards[1:]:
        loudness = loudness * one(*cut)
    return loudness


def scatter_about(own_key, extent, width, reach, shards=(), kind=jnp.bfloat16):
    values = jax.random.normal(own_key, extent, jnp.float32) * width
    if len(shards) > 0:
        values = block_levels(own_key, extent, shards, -0.22, 0.18) * values
    return jnp.clip(values, min=-reach, max=reach).astype(kind)


def setup_inputs(seed: int = 0) -> dict:
    key_of = jax.random.split(jax.random.key(seed), 5)
    queries = draw_queries(jax.random.fold_in(key_of[4], 71), 0)
    key_rows = draw_key_rows(jax.random.fold_in(key_of[4], 71), 0)
    values = scatter_about(key_of[2], (TOKENS, HD), 0.25, 4.0, ((0, 256),))
    tile_mask = draw_tile_mask(jax.random.fold_in(key_of[4], 71), 0)
    return {"queries": queries, "key_rows": key_rows, "values": values, "tile_mask": tile_mask}


masked_level = -1e30


def expand_tiles(tile_block, tile):
    tile_count = tile_block.shape[0]
    spread = jnp.broadcast_to(tile_block[:, None, :, None] > 0, (tile_count, tile, tile_count, tile))
    return spread.reshape(tile_count * tile, tile_count * tile)


def block_partial(query_block, key_block, value_block, allowed):
    score_scale = query_block.shape[-1] ** -0.5
    scores = jnp.einsum("qhd,khd->hqk", query_block.astype(jnp.float32), key_block.astype(jnp.float32)) * score_scale
    masked = jnp.where(allowed[None], scores, masked_level)
    row_peak = jnp.max(masked, axis=-1)
    weights = jnp.where(allowed[None], jnp.exp(masked - row_peak[..., None]), 0.0)
    totals = jnp.sum(weights, axis=-1)
    rounded = lax.optimization_barrier(weights.astype(jnp.bfloat16)).astype(jnp.float32)
    mixture = jnp.einsum("hqk,khd->qhd", rounded, value_block.astype(jnp.float32))
    safe_totals = jnp.maximum(totals, 1.0)
    partial_value = mixture / safe_totals.T[:, :, None]
    partial_lse = jnp.where(totals > 0, row_peak + jnp.log(safe_totals), masked_level)
    return partial_value, partial_lse


def combine_states(output, log_sums, partial_value, partial_lse):
    highest = jnp.maximum(log_sums, partial_lse)
    combined = highest + jnp.log(jnp.exp(log_sums - highest) + jnp.exp(partial_lse - highest))
    mixed_out = output * jnp.exp(log_sums - combined).T[:, :, None] + partial_value * jnp.exp(partial_lse - combined).T[:, :, None]
    return mixed_out, combined


def visit_block(carried_state, query_block, key_block, value_block, tile_mask, query_slab, key_slab):
    tile_count = query_block.shape[0] // TILE
    tile_block = lax.dynamic_slice(tile_mask, (query_slab * tile_count, key_slab * tile_count), (tile_count, tile_count))

    def include(state_pair):
        partial_value, partial_lse = block_partial(query_block, key_block, value_block, expand_tiles(tile_block, TILE))
        return combine_states(state_pair[0], state_pair[1], partial_value, partial_lse)

    def unchanged(state_pair):
        return state_pair

    return lax.cond(jnp.any(tile_block > 0), include, unchanged, carried_state)


def reference(queries, key_rows, values, tile_mask):
    query_slabs = queries.reshape(SLABS, SLAB, HEADS, HEAD_DIM)
    key_slabs = key_rows.reshape(SLABS, SLAB, HEADS, HEAD_DIM)
    value_slabs = values.reshape(SLABS, SLAB, HEADS, HEAD_DIM)

    def one_slab(slab_index):
        query_block = lax.dynamic_index_in_dim(query_slabs, slab_index, 0, keepdims=False)

        def scan_step(carried_state, offset):
            key_slab = ((slab_index + offset) % SLABS).astype(jnp.int32)
            key_block = lax.dynamic_index_in_dim(key_slabs, key_slab, 0, keepdims=False)
            value_block = lax.dynamic_index_in_dim(value_slabs, key_slab, 0, keepdims=False)
            updated = visit_block(carried_state, query_block, key_block, value_block, tile_mask, slab_index, key_slab)
            return updated, None

        initial = (jnp.zeros((SLAB, HEADS, HEAD_DIM), jnp.float32), jnp.full((HEADS, SLAB), masked_level, jnp.float32))
        finished = lax.scan(scan_step, initial, jnp.arange(SLABS, dtype=jnp.int32))[0]
        return finished[0]

    outputs = lax.map(one_slab, jnp.arange(SLABS, dtype=jnp.int32))
    return outputs.reshape(TOKENS, HD)
```

```python
import functools

import jax
import jax.numpy as jnp
from jax import lax
from jax.experimental import pallas as pl
from jax.experimental.pallas import tpu as pltpu
from jax.sharding import PartitionSpec as P

MESH = pl.DeviceIdType.MESH

HEADS = 24
HEAD_DIM = 128
TILE = 128
PIECE = 32
LEVELS = 4
HALF = 1024
QUARTER = HALF // 2
BLOCK = 256
MASKED = -1e30
SCALE2 = HEAD_DIM**-0.5 * 1.4426950408889634


def place():
    head, blk = lax.axis_index("head"), lax.axis_index("blk")
    return head // 2, blk // 8, (blk // 2) % 4, head % 2, blk % 2


def column_of(head):
    return head // 8, head % 8


def device_at(x, y, z, core):
    return (x * 2 + z % 2, y * 8 + (z // 2) * 2 + core)


def kernel(
    q_ref, k_ref, v_ref, mask_ref, out_ref,
    mask, qa, kv, hot, peak, acc, obuf,
    in_sem, in_send, self_sem, y_recv, y_send, sib_recv, sib_send, o_recv, o_send, mask_sem,
):
    x, y, zh, zl, core = place()
    z = zh * 2 + zl
    me = x * 8 + z
    busy = x < 3
    slot = (zh * 8 + x * 2 + zl) * PIECE
    up, down = (y + 1) % 4, (y + 3) % 4
    sources = (k_ref, v_ref, q_ref)

    barrier = pltpu.get_barrier_semaphore()

    def greet(i, _):
        other = (me + i) % 32
        pl.semaphore_signal(
            barrier, inc=1, device_id=device_at(other // 8, y, other % 8, core), device_id_type=MESH
        )
        return 0

    lax.fori_loop(1, 32, greet, 0)
    for there in (
        device_at(x, up, z, core), device_at(x, down, z, core), device_at(x, y, z, 1 - core),
    ):
        pl.semaphore_signal(barrier, inc=1, device_id=there, device_id_type=MESH)
    pl.semaphore_wait(barrier, 34)

    mask_copy = pltpu.make_async_copy(mask_ref, mask, mask_sem)
    mask_copy.start()

    def landing(n):
        if n == 2:
            return qa.at[pl.ds(slot, PIECE), pl.ds(0, HEAD_DIM)]
        return kv.at[n, y, core, pl.ds(slot, PIECE), :]

    for n in range(3):

        def send_piece(i, _, n=n):
            head = (me + i) % HEADS
            hx, hz = column_of(head)
            source = sources[n].at[:, pl.ds(pl.multiple_of(head * HEAD_DIM, HEAD_DIM), HEAD_DIM)]

            @pl.when(head != me)
            def _():
                pltpu.make_async_remote_copy(
                    src_ref=source, dst_ref=landing(n), send_sem=in_send.at[n], recv_sem=in_sem.at[n],
                    device_id=device_at(hx, y, hz, core), device_id_type=MESH,
                ).start()

            @pl.when(head == me)
            def _():
                pltpu.make_async_copy(source, landing(n), self_sem.at[n]).start()

            return 0

        lax.fori_loop(0, HEADS, send_piece, 0)

    def wait_pieces(n):
        whole = kv.at[0, 0, 0, pl.ds(0, HALF - PIECE), :]
        pltpu.make_async_copy(whole, whole, in_sem.at[n]).wait()
        pltpu.make_async_copy(landing(n), landing(n), self_sem.at[n]).wait()

    def y_copy(n, level, half, step, up_way):
        part = kv.at[n, level, core, pl.ds(half * QUARTER, QUARTER), :]
        return pltpu.make_async_remote_copy(
            src_ref=part, dst_ref=part, send_sem=y_send.at[n, step, half, int(up_way)],
            recv_sem=y_recv.at[n, step, half, int(up_way)],
            device_id=device_at(x, up if up_way else down, z, core), device_id_type=MESH,
        )

    def sib_copy(n, step, half, from_me=True):
        level = ((y, down, up, (y + 2) % 4))[step]
        whose = core if from_me else 1 - core
        part = kv.at[n, level, whose, pl.ds(half * QUARTER, QUARTER), :]
        return pltpu.make_async_remote_copy(
            src_ref=part, dst_ref=part, send_sem=sib_send.at[n, step, half],
            recv_sem=sib_recv.at[n, step, half],
            device_id=device_at(x, y, z, 1 - core), device_id_type=MESH,
        )

    def visit(step, whose, q_block):
        level = ((y, down, up, (y + 2) % 4))[step]
        rows = pl.ds(pl.multiple_of(q_block * BLOCK, BLOCK), BLOCK)
        keys = jnp.concatenate([kv[0, level, whose], hot[level, whose]], axis=1)
        scores = lax.dot_general(
            qa[rows, :], keys, (((1,), (1,)), ((), ())), preferred_element_type=jnp.float32
        )
        before = peak[rows, :]
        now = jnp.maximum(before, jnp.max(scores, axis=1, keepdims=True))
        peak[rows, :] = now
        weights = jnp.exp2((scores - now[:, :1]) * SCALE2).astype(jnp.bfloat16)
        fade = jnp.exp2((before - now) * SCALE2)
        vals = jnp.concatenate(
            [kv[1, level, whose], jnp.ones((HALF, HEAD_DIM), jnp.bfloat16)], axis=1
        )
        mixed = jnp.dot(weights, vals, preferred_element_type=jnp.float32)
        acc[rows, :] = acc[rows, :] * jnp.concatenate([fade, fade], axis=1) + mixed

    def visit_all(step, whose):
        def one(q_block, _):
            visit(step, whose, q_block)
            return 0

        lax.fori_loop(0, HALF // BLOCK, one, 0)

    @pl.when(busy)
    def _():
        lane = lax.broadcasted_iota(jnp.int32, (HALF, TILE), 1)
        row = lax.broadcasted_iota(jnp.int32, (HALF, TILE), 0)
        for level in range(LEVELS):
            for c in range(2):
                tile = level * 16 + (row // BLOCK) * 4 + c * 2 + (row // TILE) % 2
                hot[level, c] = jnp.where(lane == tile, 1.0, 0.0).astype(jnp.bfloat16)
        mask_copy.wait()
        for t in range(8):
            q_tile = y * 16 + (t // 2) * 4 + core * 2 + t % 2
            allowed = mask[pl.ds(q_tile, 1), :]
            bias = jnp.where(allowed > 0, 0.0, MASKED)
            bias = jnp.concatenate([bias, jnp.zeros_like(bias)], axis=1)
            qa[pl.ds(t * TILE, TILE), pl.ds(HEAD_DIM, TILE)] = jnp.broadcast_to(
                bias, (TILE, TILE)
            ).astype(jnp.bfloat16)
        peak[...] = jnp.full(peak.shape, MASKED, jnp.float32)
        acc[...] = jnp.zeros(acc.shape, jnp.float32)

        for n in range(2):
            wait_pieces(n)
            y_copy(n, y, 0, 0, True).start()
            y_copy(n, y, 1, 0, False).start()
            y_copy(n, y, 1, 0, True).start()
            y_copy(n, y, 0, 0, False).start()
            sib_copy(n, 0, 0).start()
            sib_copy(n, 0, 1).start()
        wait_pieces(2)
        visit_all(0, core)

        def pass_on(n):
            y_copy(n, down, 0, 0, True).wait_recv()
            y_copy(n, down, 0, 1, True).start()
            sib_copy(n, 1, 0).start()
            y_copy(n, up, 1, 0, False).wait_recv()
            y_copy(n, up, 1, 1, False).start()
            sib_copy(n, 2, 1).start()
            y_copy(n, down, 1, 0, True).wait_recv()
            sib_copy(n, 1, 1).start()
            y_copy(n, up, 0, 0, False).wait_recv()
            sib_copy(n, 2, 0).start()

        def wait_sibling(step):
            for n in range(2):
                for half in range(2):
                    sib_copy(n, step, half, False).wait_recv()

        pass_on(0)
        wait_sibling(0)
        visit_all(0, 1 - core)
        pass_on(1)
        near_down, near_up = y != 0, y != 3

        @pl.when(near_down)
        def _():
            visit_all(1, core)

        @pl.when(near_up)
        def _():
            visit_all(2, core)

        wait_sibling(1)

        @pl.when(near_down)
        def _():
            visit_all(1, 1 - core)

        wait_sibling(2)

        @pl.when(near_up)
        def _():
            visit_all(2, 1 - core)

        far = (y + 2) % 4
        for n in range(2):
            y_copy(n, far, 0, 1, True).wait_recv()
            sib_copy(n, 3, 0).start()
            y_copy(n, far, 1, 1, False).wait_recv()
            sib_copy(n, 3, 1).start()
        visit_all(3, core)
        wait_sibling(3)

        def finish(q_block, _):
            visit(3, 1 - core, q_block)
            rows = pl.ds(pl.multiple_of(q_block * BLOCK, BLOCK), BLOCK)
            obuf[rows, :] = acc[rows, :HEAD_DIM] / acc[rows, HEAD_DIM:]

            def send_back(there, _):
                piece = q_block * 8 + there
                source = obuf.at[pl.ds(pl.multiple_of(piece * PIECE, PIECE), PIECE), :]
                target = out_ref.at[:, pl.ds(pl.multiple_of(me * HEAD_DIM, HEAD_DIM), HEAD_DIM)]
                mine = (q_block == zh) & (there == x * 2 + zl)

                @pl.when(jnp.logical_not(mine))
                def _():
                    pltpu.make_async_remote_copy(
                        src_ref=source, dst_ref=target, send_sem=o_send, recv_sem=o_recv,
                        device_id=(there, y * 8 + q_block * 2 + core), device_id_type=MESH,
                    ).start()

                @pl.when(mine)
                def _():
                    pltpu.make_async_copy(source, target, self_sem.at[3]).start()

                return 0

            lax.fori_loop(0, 8, send_back, 0)
            return 0

        lax.fori_loop(0, HALF // BLOCK, finish, 0)

        for n in range(2):
            for half in range(2):
                for way in (True, False):
                    y_copy(n, y, half, 0, way).wait_send()
                for step in range(4):
                    sib_copy(n, step, half).wait_send()
            y_copy(n, down, 0, 1, True).wait_send()
            y_copy(n, up, 1, 1, False).wait_send()
        sent = obuf.at[pl.ds(0, HALF - PIECE), :]
        pltpu.make_async_copy(sent, sent, o_send).wait()

    @pl.when(busy)
    def _():
        others = out_ref.at[:, pl.ds(0, (HEADS - 1) * HEAD_DIM)]
        one = out_ref.at[:, pl.ds(0, HEAD_DIM)]
        sent = q_ref.at[:, pl.ds(0, (HEADS - 1) * HEAD_DIM)]
        for n in range(3):
            pltpu.make_async_copy(sent, sent, in_send.at[n]).wait()
        pltpu.make_async_copy(one, one, self_sem.at[3]).wait()
        pltpu.make_async_copy(others, others, o_recv).wait()

    @pl.when(jnp.logical_not(busy))
    def _():
        for n in range(3):
            pltpu.make_async_copy(q_ref, q_ref, in_send.at[n]).wait()
        pltpu.make_async_copy(out_ref, out_ref, o_recv).wait()
        mask_copy.wait()


def local(queries, key_rows, values, tile_mask):
    bf16, f32, dma = jnp.bfloat16, jnp.float32, pltpu.SemaphoreType.DMA
    return pl.pallas_call(
        kernel,
        out_shape=jax.ShapeDtypeStruct(queries.shape, f32),
        in_specs=[pl.BlockSpec(memory_space=pltpu.HBM)] * 4,
        out_specs=pl.BlockSpec(memory_space=pltpu.VMEM),
        scratch_shapes=[
            pltpu.VMEM(tile_mask.shape, jnp.int32),
            pltpu.VMEM((HALF, 2 * HEAD_DIM), bf16),
            pltpu.VMEM((2, LEVELS, 2, HALF, HEAD_DIM), bf16),
            pltpu.VMEM((LEVELS, 2, HALF, TILE), bf16),
            pltpu.VMEM((HALF, HEAD_DIM), f32),
            pltpu.VMEM((HALF, 2 * HEAD_DIM), f32),
            pltpu.VMEM((HALF, HEAD_DIM), f32),
            dma((3,)),
            dma((3,)),
            dma((4,)),
            dma((2, 2, 2, 2)),
            dma((2, 2, 2, 2)),
            dma((2, 4, 2)),
            dma((2, 4, 2)),
            dma,
            dma,
            dma,
        ],
        compiler_params=pltpu.CompilerParams(
            collective_id=0, has_side_effects=True, vmem_limit_bytes=48 * 2**20
        ),
    )(queries, key_rows, values, tile_mask)


def solution(mesh):
    return jax.shard_map(
        local,
        mesh=mesh,
        in_specs=(
            P(("blk", "head"), None),
            P(("blk", "head"), None),
            P(("blk", "head"), None),
            P(),
        ),
        out_specs=P(("blk", "head"), None),
        check_vma=False,
    )
```

```python
import jax
import jax.numpy as jnp
from jax import lax
from jax.experimental import pallas as pl
from jax.experimental.pallas import tpu as pltpu
from jax.sharding import PartitionSpec as P

MESH = pl.DeviceIdType.MESH

HEADS = 24
HEAD_DIM = 128
TILE = 128
PIECE = 32
LEVELS = 4
HALF = 1024
SLAB = 256
ORDER = (0, 1, 3, 2)
GOES_UP = (0, 3)
MASKED = -1e30
SCALE2 = HEAD_DIM**-0.5 * 1.4426950408889634


def place():
    head, blk = lax.axis_index("head"), lax.axis_index("blk")
    return head // 2, blk // 8, (blk // 2) % 4, head % 2, blk % 2


def column_of(head):
    return head // 8, head % 8


def device_at(x, y, z, core):
    return (x * 2 + z % 2, y * 8 + (z // 2) * 2 + core)


def span(r):
    return max(0, r - 2) * SLAB, (min(3, r + 2) + 1) * SLAB


def kernel(
    q_ref, k_ref, v_ref, mask_ref, out_ref,
    mask, qa, kv, wbuf, peaks, totals, gains, acc, obuf,
    in_sem, in_send, self_sem, y_recv, y_send, sib_recv, sib_send, o_recv, o_send, mask_sem,
):
    x, y, zh, zl, core = place()
    z = zh * 2 + zl
    me = x * 8 + z
    busy = x < 3
    slot = (zh * 8 + x * 2 + zl) * PIECE
    up, down, far = (y + 1) % 4, (y + 3) % 4, (y + 2) % 4
    levels = (y, down, up, far)
    sources = (k_ref, v_ref, q_ref)

    barrier = pltpu.get_barrier_semaphore()

    def greet(i, _):
        other = (me + i) % 32
        pl.semaphore_signal(
            barrier, inc=1, device_id=device_at(other // 8, y, other % 8, core), device_id_type=MESH
        )
        return 0

    lax.fori_loop(1, 32, greet, 0)
    for there in (
        device_at(x, up, z, core), device_at(x, down, z, core), device_at(x, y, z, 1 - core),
    ):
        pl.semaphore_signal(barrier, inc=1, device_id=there, device_id_type=MESH)
    with jax.named_scope("barrier"):
        pl.semaphore_wait(barrier, 34)

    def landing(n):
        if n == 2:
            return qa.at[pl.ds(slot, PIECE), pl.ds(0, HEAD_DIM)]
        return kv.at[n, y, core, pl.ds(slot, PIECE), :]

    def slab_rows(rel):
        return pl.ds(pl.multiple_of((zh + rel) % 4 * SLAB, SLAB), SLAB)

    def send_pieces(n):
        def send_piece(i, _):
            turn, w = i // 6, i % 6
            off = jnp.where(turn < 2, turn, 5 - turn)
            hz = (zh + off) % 4 * 2 + w % 2
            hx = (x + w // 2) % 3
            head = hx * 8 + hz
            source = sources[n].at[:, pl.ds(pl.multiple_of(head * HEAD_DIM, HEAD_DIM), HEAD_DIM)]

            @pl.when(head != me)
            def _():
                pltpu.make_async_remote_copy(
                    src_ref=source, dst_ref=landing(n), send_sem=in_send.at[n],
                    recv_sem=in_sem.at[n, (4 - off) % 4],
                    device_id=device_at(hx, y, hz, core), device_id_type=MESH,
                ).start()

            @pl.when(head == me)
            def _():
                pltpu.make_async_copy(source, landing(n), self_sem.at[n]).start()

            return 0

        lax.fori_loop(0, HEADS, send_piece, 0)

    with jax.named_scope("pieces out"):
        send_pieces(0)
        send_pieces(2)
        send_pieces(1)
    mask_copy = pltpu.make_async_copy(mask_ref, mask, mask_sem)
    mask_copy.start()

    def wait_slab(n, rel):
        if rel == 0:
            part = kv.at[0, 0, 0, pl.ds(0, SLAB - PIECE), :]
            pltpu.make_async_copy(part, part, in_sem.at[n, 0]).wait()
            pltpu.make_async_copy(landing(n), landing(n), self_sem.at[n]).wait()
        else:
            part = kv.at[0, 0, 0, pl.ds(0, SLAB), :]
            pltpu.make_async_copy(part, part, in_sem.at[n, rel]).wait()

    def y_copy(n, level, rel, step, up_way):
        part = kv.at[n, level, core, slab_rows(rel), :]
        return pltpu.make_async_remote_copy(
            src_ref=part, dst_ref=part, send_sem=y_send.at[n, step, rel, int(up_way)],
            recv_sem=y_recv.at[n, step, rel, int(up_way)],
            device_id=device_at(x, up if up_way else down, z, core), device_id_type=MESH,
        )

    def sib_copy(n, step, rel, from_me=True):
        whose = core if from_me else 1 - core
        part = kv.at[n, levels[step], whose, slab_rows(rel), :]
        return pltpu.make_async_remote_copy(
            src_ref=part, dst_ref=part, send_sem=sib_send.at[n, step, rel],
            recv_sem=sib_recv.at[n, step, rel],
            device_id=device_at(x, y, z, 1 - core), device_id_type=MESH,
        )

    def own_slab(n, rel):
        wait_slab(n, rel)
        y_copy(n, y, rel, 0, True).start()
        y_copy(n, y, rel, 0, False).start()
        sib_copy(n, 0, rel).start()

    def next_slab(n, rel):
        y_copy(n, down, rel, 0, True).wait_recv()
        if rel in GOES_UP:
            y_copy(n, down, rel, 1, True).start()
        sib_copy(n, 1, rel).start()
        y_copy(n, up, rel, 0, False).wait_recv()
        if rel not in GOES_UP:
            y_copy(n, up, rel, 1, False).start()
        sib_copy(n, 2, rel).start()

    def far_slab(n, rel):
        y_copy(n, far, rel, 1, rel in GOES_UP).wait_recv()
        sib_copy(n, 3, rel).start()

    def from_sibling(n, step):
        for rel in range(4):
            sib_copy(n, step, rel, False).wait_recv()

    def turn(i):
        step = i // 2
        off = jnp.where(step == 0, 0, jnp.where(step == 1, 3, jnp.where(step == 2, 1, 2)))
        return (y + off) % 4, (core + i) % 2

    def weigh(i, block=None):
        level, whose = turn(i)
        for r in range(4):
            lo, hi = span(r)
            rows = pl.ds(lo, hi - lo) if block is None else block
            lane = lax.broadcasted_iota(jnp.int32, (SLAB, TILE), 1)
            row = lax.broadcasted_iota(jnp.int32, (SLAB, TILE), 0)
            hot = lane == level * 16 + r * 4 + whose * 2 + row // TILE
            keys = jnp.concatenate(
                [
                    kv[0, level, whose, r * SLAB : (r + 1) * SLAB, :],
                    jnp.where(hot, 1.0, 0.0).astype(jnp.bfloat16),
                ],
                axis=1,
            )
            scores = lax.dot_general(
                qa[rows, :], keys, (((1,), (1,)), ((), ())), preferred_element_type=jnp.float32
            )
            peak = jnp.max(scores, axis=1, keepdims=True)
            weights = jnp.exp2((scores - peak) * SCALE2)
            wbuf[i, rows, r * SLAB : (r + 1) * SLAB] = weights.astype(jnp.bfloat16)
            before = peaks[rows, :]
            here = lax.broadcasted_iota(jnp.int32, before.shape, 1) == i * 4 + r
            peaks[rows, :] = jnp.where(here, peak, before)

    def mix(i, first=0, last=HALF):
        level, whose = turn(i)
        for r in range(4):
            lo, hi = max(span(r)[0], first), min(span(r)[1], last)
            if lo >= hi:
                continue
            rows = pl.ds(lo, hi - lo)
            lane = lax.broadcasted_iota(jnp.int32, (SLAB, TILE), 1)
            vals = jnp.concatenate(
                [
                    kv[1, level, whose, r * SLAB : (r + 1) * SLAB, :],
                    jnp.where(lane == i * 4 + r, 1.0, 0.0).astype(jnp.bfloat16),
                ],
                axis=1,
            )
            mixed = jnp.dot(
                wbuf[i, rows, r * SLAB : (r + 1) * SLAB], vals, preferred_element_type=jnp.float32
            )
            gain = gains[rows, :]
            here = lax.broadcasted_iota(jnp.int32, gain.shape, 1) == i * 4 + r
            gain = jnp.sum(jnp.where(here, gain, 0.0), axis=1, keepdims=True)
            acc[rows, :] += mixed[:, :HEAD_DIM] * gain
            totals[rows, :] += mixed[:, HEAD_DIM:]

    def near(i):
        level, _ = turn(i)
        return jnp.abs(level - y) < 3

    @pl.when(busy)
    def _():
        mask_copy.wait()
        for t in range(8):
            q_tile = y * 16 + (t // 2) * 4 + core * 2 + t % 2
            allowed = mask[pl.ds(q_tile, 1), :]
            bias = jnp.where(allowed > 0, 0.0, MASKED)
            bias = jnp.concatenate([bias, jnp.zeros_like(bias)], axis=1)
            qa[pl.ds(t * TILE, TILE), pl.ds(HEAD_DIM, TILE)] = jnp.broadcast_to(
                bias, (TILE, TILE)
            ).astype(jnp.bfloat16)
        peaks[...] = jnp.full(peaks.shape, MASKED, jnp.float32)
        totals[...] = jnp.zeros(totals.shape, jnp.float32)
        acc[...] = jnp.zeros(acc.shape, jnp.float32)

        with jax.named_scope("own keys"):
            own_slab(0, 0)
            own_slab(0, 1)
            own_slab(0, 3)
        with jax.named_scope("first next keys"):
            next_slab(0, 0)
            own_slab(0, 2)
        with jax.named_scope("next keys"):
            next_slab(0, 1)

        def weigh_own(k, _):
            for n, rel in enumerate(ORDER):

                @pl.when(k == n)
                def _(rel=rel):
                    with jax.named_scope("query slab"):
                        wait_slab(2, rel)

            @pl.when(k == 0)
            def _():
                with jax.named_scope("sibling keys"):
                    from_sibling(0, 0)

            @pl.when(k == 2)
            def _():
                with jax.named_scope("next keys"):
                    next_slab(0, 3)

            @pl.when(k == 3)
            def _():
                with jax.named_scope("next keys"):
                    next_slab(0, 2)

            rows = slab_rows(jnp.where(k < 2, k, 5 - k))
            with jax.named_scope("weigh own"):
                weigh(0, rows)
                weigh(1, rows)
            return 0

        lax.fori_loop(0, 4, weigh_own, 0)

        hooks = {
            2: (lambda: own_slab(1, 0),),
            3: (lambda: own_slab(1, 1), lambda: from_sibling(0, 1)),
            4: (lambda: own_slab(1, 3), lambda: far_slab(0, 0), lambda: far_slab(0, 1)),
            5: (lambda: own_slab(1, 2), lambda: next_slab(1, 0), lambda: from_sibling(0, 2)),
            6: (lambda: far_slab(0, 3), lambda: far_slab(0, 2), lambda: next_slab(1, 1)),
            7: (lambda: next_slab(1, 3), lambda: from_sibling(0, 3)),
        }

        def weigh_turn(i, _):
            for at, calls in hooks.items():

                @pl.when(i == at)
                def _(calls=calls):
                    with jax.named_scope("between weighings"):
                        for call in calls:
                            call()

            @pl.when(near(i))
            def _():
                with jax.named_scope("weigh"):
                    weigh(i)

            return 0

        lax.fori_loop(2, 8, weigh_turn, 0)
        every = peaks[...]
        gains[...] = jnp.exp2((every - jnp.max(every, axis=1, keepdims=True)) * SCALE2)

        mix_hooks = {
            0: (lambda: next_slab(1, 2),),
            1: (lambda: from_sibling(1, 0),),
            2: (lambda: far_slab(1, 0),),
            3: (lambda: far_slab(1, 1), lambda: from_sibling(1, 1)),
            4: (lambda: far_slab(1, 3),),
            5: (lambda: far_slab(1, 2), lambda: from_sibling(1, 2)),
        }

        def mix_turn(i, _):
            for at, calls in mix_hooks.items():

                @pl.when(i == at)
                def _(calls=calls):
                    with jax.named_scope("between mixings"):
                        for call in calls:
                            call()

            @pl.when(near(i))
            def _():
                with jax.named_scope("mix"):
                    mix(i)

            return 0

        lax.fori_loop(0, 6, mix_turn, 0)
        with jax.named_scope("last sibling values"):
            from_sibling(1, 3)

        for q_block in range(HALF // SLAB):
            rows = pl.ds(q_block * SLAB, SLAB)
            with jax.named_scope("last mix"):
                for i in (6, 7):
                    mix(i, q_block * SLAB, (q_block + 1) * SLAB)
                total = jnp.sum(totals[rows, :] * gains[rows, :], axis=1, keepdims=True)
                obuf[rows, :] = (acc[rows, :] / total).astype(jnp.bfloat16)

            def send_back(there, _, q_block=q_block):
                piece = q_block * 8 + there
                source = obuf.at[pl.ds(pl.multiple_of(piece * PIECE, PIECE), PIECE), :]
                target = out_ref.at[:, pl.ds(pl.multiple_of(me * HEAD_DIM, HEAD_DIM), HEAD_DIM)]
                mine = (q_block == zh) & (there == x * 2 + zl)

                @pl.when(jnp.logical_not(mine))
                def _():
                    pltpu.make_async_remote_copy(
                        src_ref=source, dst_ref=target, send_sem=o_send, recv_sem=o_recv,
                        device_id=(there, y * 8 + q_block * 2 + core), device_id_type=MESH,
                    ).start()

                @pl.when(mine)
                def _():
                    pltpu.make_async_copy(source, target, self_sem.at[3]).start()

                return 0

            lax.fori_loop(0, 8, send_back, 0)

        for n in range(2):
            for rel in range(4):
                for way in (True, False):
                    y_copy(n, y, rel, 0, way).wait_send()
                for step in range(4):
                    sib_copy(n, step, rel).wait_send()
                if rel in GOES_UP:
                    y_copy(n, down, rel, 1, True).wait_send()
                else:
                    y_copy(n, up, rel, 1, False).wait_send()
        others = out_ref.at[:, pl.ds(0, (HEADS - 1) * HEAD_DIM)]
        for n in range(3):
            pltpu.make_async_copy(others, others, in_send.at[n]).wait()
        sent = obuf.at[pl.ds(0, HALF - PIECE), :]
        with jax.named_scope("output sent"):
            pltpu.make_async_copy(sent, sent, o_send).wait()
        one = out_ref.at[:, pl.ds(0, HEAD_DIM)]
        pltpu.make_async_copy(one, one, self_sem.at[3]).wait()
        with jax.named_scope("output here"):
            pltpu.make_async_copy(others, others, o_recv).wait()

    @pl.when(jnp.logical_not(busy))
    def _():
        mask_copy.wait()
        for n in range(3):
            pltpu.make_async_copy(out_ref, out_ref, in_send.at[n]).wait()
        pltpu.make_async_copy(out_ref, out_ref, o_recv).wait()


def local(queries, key_rows, values, tile_mask):
    bf16, f32, dma = jnp.bfloat16, jnp.float32, pltpu.SemaphoreType.DMA
    queries, key_rows, values, tile_mask = (
        pltpu.with_memory_space_constraint(a, pltpu.HBM) for a in (queries, key_rows, values, tile_mask)
    )
    gathered = pl.pallas_call(
        kernel,
        out_shape=jax.ShapeDtypeStruct(queries.shape, bf16),
        in_specs=[pl.BlockSpec(memory_space=pltpu.HBM)] * 4,
        out_specs=pl.BlockSpec(memory_space=pltpu.VMEM),
        scratch_shapes=[
            pltpu.VMEM(tile_mask.shape, jnp.int32),
            pltpu.VMEM((HALF, 2 * HEAD_DIM), bf16),
            pltpu.VMEM((2, LEVELS, 2, HALF, HEAD_DIM), bf16),
            pltpu.VMEM((8, HALF, HALF), bf16),
            pltpu.VMEM((HALF, TILE), f32),
            pltpu.VMEM((HALF, TILE), f32),
            pltpu.VMEM((HALF, TILE), f32),
            pltpu.VMEM((HALF, HEAD_DIM), f32),
            pltpu.VMEM((HALF, HEAD_DIM), bf16),
            dma((3, 4)),
            dma((3,)),
            dma((4,)),
            dma((2, 2, 4, 2)),
            dma((2, 2, 4, 2)),
            dma((2, 4, 4)),
            dma((2, 4, 4)),
            dma,
            dma,
            dma,
        ],
        compiler_params=pltpu.CompilerParams(
            collective_id=0, has_side_effects=True, vmem_limit_bytes=48 * 2**20
        ),
    )(queries, key_rows, values, tile_mask)
    return gathered.astype(f32)


def solution(mesh):
    return jax.shard_map(
        local,
        mesh=mesh,
        in_specs=(
            P(("blk", "head"), None),
            P(("blk", "head"), None),
            P(("blk", "head"), None),
            P(),
        ),
        out_specs=P(("blk", "head"), None),
        check_vma=False,
    )
```

```python
import jax
import jax.numpy as jnp
from jax import lax
from jax.experimental import pallas as pl
from jax.experimental.pallas import tpu as pltpu
from jax.sharding import PartitionSpec as P

MESH = pl.DeviceIdType.MESH

HEADS = 24
HEAD_DIM = 128
TILE = 128
PIECE = 32
LEVELS = 4
HALF = 1024
SLAB = 256
ORDER = (0, 1, 3, 2)
GOES_UP = (0, 3)
MASKED = -1e30
SCALE2 = HEAD_DIM**-0.5 * 1.4426950408889634


def place():
    head, blk = lax.axis_index("head"), lax.axis_index("blk")
    return head // 2, blk // 8, (blk // 2) % 4, head % 2, blk % 2


def column_of(head):
    return head // 8, head % 8


def device_at(x, y, z, core):
    return (x * 2 + z % 2, y * 8 + (z // 2) * 2 + core)


def span(r):
    return max(0, r - 2) * SLAB, (min(3, r + 2) + 1) * SLAB


def kernel(
    q_ref, k_ref, v_ref, mask_ref, out_ref,
    mask, rows_in, qa, kv, wbuf, peaks, totals, gains, acc, obuf,
    in_sem, in_send, self_sem, y_recv, y_send, sib_recv, sib_send, o_recv, o_send, mask_sem, load_sem,
):
    x, y, zh, zl, core = place()
    z = zh * 2 + zl
    me = x * 8 + z
    busy = x < 3
    slot = (zh * 8 + x * 2 + zl) * PIECE
    up, down, far = (y + 1) % 4, (y + 3) % 4, (y + 2) % 4
    levels = (y, down, up, far)
    sources = (rows_in.at[0], rows_in.at[1], rows_in.at[2])
    loads = [
        pltpu.make_async_copy(ref, rows_in.at[n], load_sem.at[n])
        for n, ref in enumerate((k_ref, v_ref, q_ref))
    ]
    for n in (0, 2, 1):
        loads[n].start()

    mask_copy = pltpu.make_async_copy(mask_ref, mask, mask_sem)
    mask_copy.start()
    barrier = pltpu.get_barrier_semaphore()

    def greet(i, _):
        hx, hz = i // 8, (z + i) % 8

        @pl.when((hx * 8 + hz != me) & (busy | (hx < 3)))
        def _():
            pl.semaphore_signal(
                barrier, inc=1, device_id=device_at(hx, y, hz, core), device_id_type=MESH
            )

        return 0

    lax.fori_loop(0, 32, greet, 0)

    @pl.when(busy)
    def _():
        for there in (
            device_at(x, up, z, core), device_at(x, down, z, core), device_at(x, y, z, 1 - core),
        ):
            pl.semaphore_signal(barrier, inc=1, device_id=there, device_id_type=MESH)

    @pl.when(busy)
    def _():
        mask_copy.wait()
        for t in range(8):
            q_tile = y * 16 + (t // 2) * 4 + core * 2 + t % 2
            allowed = mask[pl.ds(q_tile, 1), :]
            bias = jnp.where(allowed > 0, 0.0, MASKED)
            bias = jnp.concatenate([bias, jnp.zeros_like(bias)], axis=1)
            qa[pl.ds(t * TILE, TILE), pl.ds(HEAD_DIM, TILE)] = jnp.broadcast_to(
                bias, (TILE, TILE)
            ).astype(jnp.bfloat16)
        peaks[...] = jnp.full(peaks.shape, MASKED, jnp.float32)
        totals[...] = jnp.zeros(totals.shape, jnp.float32)
        acc[...] = jnp.zeros(acc.shape, jnp.float32)

        wbuf[7, pl.ds(0, SLAB), pl.ds(3 * SLAB, SLAB)] = jnp.zeros((SLAB, SLAB), jnp.bfloat16)
        wbuf[7, pl.ds(3 * SLAB, SLAB), pl.ds(0, SLAB)] = jnp.zeros((SLAB, SLAB), jnp.bfloat16)

    with jax.named_scope("barrier"):
        @pl.when(busy)
        def _():
            pl.semaphore_wait(barrier, 34)

        @pl.when(jnp.logical_not(busy))
        def _():
            pl.semaphore_wait(barrier, HEADS)


    def landing(n):
        if n == 2:
            return qa.at[pl.ds(slot, PIECE), pl.ds(0, HEAD_DIM)]
        return kv.at[n, y, core, pl.ds(slot, PIECE), :]

    def slab_rows(rel):
        return pl.ds(pl.multiple_of((zh + rel) % 4 * SLAB, SLAB), SLAB)

    def send_pieces(n):
        def send_piece(i, _):
            turn, w = i // 6, i % 6
            off = jnp.where(turn < 2, turn, 5 - turn)
            hz = (zh + off) % 4 * 2 + w % 2
            hx = (x + w // 2) % 3
            head = hx * 8 + hz
            source = sources[n].at[:, pl.ds(pl.multiple_of(head * HEAD_DIM, HEAD_DIM), HEAD_DIM)]

            @pl.when(head != me)
            def _():
                pltpu.make_async_remote_copy(
                    src_ref=source, dst_ref=landing(n), send_sem=in_send.at[n],
                    recv_sem=in_sem.at[n, (4 - off) % 4],
                    device_id=device_at(hx, y, hz, core), device_id_type=MESH,
                ).start()

            @pl.when(head == me)
            def _():
                pltpu.make_async_copy(source, landing(n), self_sem.at[n]).start()

            return 0

        lax.fori_loop(0, HEADS, send_piece, 0)

    with jax.named_scope("pieces out"):
        for n in (0, 2, 1):
            loads[n].wait()
            send_pieces(n)

    def wait_slab(n, rel):
        if rel == 0:
            part = kv.at[0, 0, 0, pl.ds(0, SLAB - PIECE), :]
            pltpu.make_async_copy(part, part, in_sem.at[n, 0]).wait()
            pltpu.make_async_copy(landing(n), landing(n), self_sem.at[n]).wait()
        else:
            part = kv.at[0, 0, 0, pl.ds(0, SLAB), :]
            pltpu.make_async_copy(part, part, in_sem.at[n, rel]).wait()

    def y_copy(n, level, rel, way):
        part = kv.at[n, level, core, slab_rows(rel), :]
        upward = rel in GOES_UP if way == 2 else way == 0
        return pltpu.make_async_remote_copy(
            src_ref=part, dst_ref=part, send_sem=y_send, recv_sem=y_recv.at[n, way, rel],
            device_id=device_at(x, up if upward else down, z, core), device_id_type=MESH,
        )

    def to_sibling(n, step, rel=None):
        part = kv.at[n, levels[step], core]
        if rel is not None:
            part = part.at[slab_rows(rel), :]
        pltpu.make_async_remote_copy(
            src_ref=part, dst_ref=part, send_sem=sib_send, recv_sem=sib_recv.at[n, step],
            device_id=device_at(x, y, z, 1 - core), device_id_type=MESH,
        ).start()

    def own_slab(n, rel):
        wait_slab(n, rel)
        y_copy(n, y, rel, 0).start()
        y_copy(n, y, rel, 1).start()
        if rel == ORDER[-1]:
            to_sibling(n, 0)

    def next_slab(n, rel):
        y_copy(n, down, rel, 0).wait_recv()
        if rel in GOES_UP:
            y_copy(n, down, rel, 2).start()
        y_copy(n, up, rel, 1).wait_recv()
        if rel not in GOES_UP:
            y_copy(n, up, rel, 2).start()
        if rel == ORDER[-1]:
            to_sibling(n, 1)
            to_sibling(n, 2)

    def far_slab(n, rel):
        y_copy(n, far, rel, 2).wait_recv()
        if n == 1:
            to_sibling(n, 3, rel)
        elif rel == ORDER[-1]:
            to_sibling(n, 3)

    def from_sibling(n, step):
        part = kv.at[n, levels[step], 1 - core]
        pltpu.make_async_copy(part, part, sib_recv.at[n, step]).wait()

    def turn(i):
        step = i // 2
        off = jnp.where(step == 0, 0, jnp.where(step == 1, 3, jnp.where(step == 2, 1, 2)))
        return (y + off) % 4, (core + i) % 2

    def weigh(i, block=None):
        level, whose = turn(i)
        for r in range(4):
            lo, hi = span(r)
            rows = pl.ds(lo, hi - lo) if block is None else block
            lane = lax.broadcasted_iota(jnp.int32, (SLAB, TILE), 1)
            row = lax.broadcasted_iota(jnp.int32, (SLAB, TILE), 0)
            hot = lane == level * 16 + r * 4 + whose * 2 + row // TILE
            keys = jnp.concatenate(
                [
                    kv[0, level, whose, r * SLAB : (r + 1) * SLAB, :],
                    jnp.where(hot, 1.0, 0.0).astype(jnp.bfloat16),
                ],
                axis=1,
            )
            scores = lax.dot_general(
                qa[rows, :], keys, (((1,), (1,)), ((), ())), preferred_element_type=jnp.float32
            )
            peak = jnp.max(scores, axis=1, keepdims=True)
            weights = jnp.exp2((scores - peak) * SCALE2)
            wbuf[i, rows, r * SLAB : (r + 1) * SLAB] = weights.astype(jnp.bfloat16)
            before = peaks[rows, :]
            here = lax.broadcasted_iota(jnp.int32, before.shape, 1) == i * 4 + r
            peaks[rows, :] = jnp.where(here, peak, before)

    def mix(i, block=None):
        level, whose = turn(i)
        for r in range(4):
            lo, hi = span(r)
            rows = pl.ds(lo, hi - lo) if block is None else block
            lane = lax.broadcasted_iota(jnp.int32, (SLAB, TILE), 1)
            vals = jnp.concatenate(
                [
                    kv[1, level, whose, r * SLAB : (r + 1) * SLAB, :],
                    jnp.where(lane == i * 4 + r, 1.0, 0.0).astype(jnp.bfloat16),
                ],
                axis=1,
            )
            mixed = jnp.dot(
                wbuf[i, rows, r * SLAB : (r + 1) * SLAB], vals, preferred_element_type=jnp.float32
            )
            gain = gains[rows, :]
            here = lax.broadcasted_iota(jnp.int32, gain.shape, 1) == i * 4 + r
            gain = jnp.sum(jnp.where(here, gain, 0.0), axis=1, keepdims=True)
            acc[rows, :] += mixed[:, :HEAD_DIM] * gain
            totals[rows, :] += mixed[:, HEAD_DIM:]

    def near(i):
        level, _ = turn(i)
        return jnp.abs(level - y) < 3

    @pl.when(busy)
    def _():
        own_slab(0, 0)
        own_slab(0, 1)
        own_slab(0, 3)
        own_slab(0, 2)
        next_slab(0, 0)
        next_slab(0, 1)

        def run_hooks(hooks, i):
            if isinstance(i, int):
                for call, n, which in hooks.get(i, ()):
                    call(n, which)
                return
            for at, calls in hooks.items():

                @pl.when(i == at)
                def _(calls=calls):
                    for call, n, which in calls:
                        call(n, which)

        own_hooks = {
            0: ((wait_slab, 2, 0), (wait_slab, 2, 1)),
            1: ((next_slab, 0, 3), (from_sibling, 0, 0)),
            2: ((next_slab, 0, 2), (wait_slab, 2, 3), (wait_slab, 2, 2)),
            3: ((own_slab, 1, 0),),
        }

        def weigh_own(j, _):
            run_hooks(own_hooks, j)
            with jax.named_scope("weigh own"):
                for k in range(2):
                    weigh(j % 2, slab_rows(jnp.where(j < 2, k, 3 - k)))
            return 0

        lax.fori_loop(0, 4, weigh_own, 0)

        weigh_hooks = {
            2: ((own_slab, 1, 1),),
            3: ((own_slab, 1, 3), (from_sibling, 0, 1)),
            4: ((own_slab, 1, 2), (far_slab, 0, 0), (far_slab, 0, 1), (far_slab, 0, 3), (far_slab, 0, 2)),
            5: ((from_sibling, 0, 2),),
            6: ((next_slab, 1, 0),),
            7: ((next_slab, 1, 1), (from_sibling, 0, 3)),
        }
        mix_hooks = {
            0: ((next_slab, 1, 3),),
            1: ((next_slab, 1, 2), (from_sibling, 1, 0)),
            3: ((far_slab, 1, 0),),
            4: ((far_slab, 1, 1), (from_sibling, 1, 1)),
            5: ((from_sibling, 1, 2), (far_slab, 1, 3)),
            6: ((far_slab, 1, 2),),
        }

        def weigh_turn(i, _):
            run_hooks(weigh_hooks, i)

            def _():
                with jax.named_scope("weigh"):
                    weigh(i)

            _() if i > 5 else pl.when(near(i))(_)

            return 0

        for i in range(2, 8):
            weigh_turn(i, 0)
        every = peaks[...]
        gains[...] = jnp.exp2((every - jnp.max(every, axis=1, keepdims=True)) * SCALE2)

        def mix_turn(m, _):
            run_hooks(mix_hooks, m)
            i = (0, 1, 2, 4, 3, 5, 6)[m]

            def _():
                with jax.named_scope("mix"):
                    mix(i)

            _() if i > 5 or i < 2 else pl.when(near(i))(_)

            return 0

        for m in range(7):
            mix_turn(m, 0)
        from_sibling(1, 3)

        def finish(q_block, _):
            rows = pl.ds(pl.multiple_of(q_block * SLAB, SLAB), SLAB)
            with jax.named_scope("last mix"):
                mix(7, rows)
                total = jnp.sum(totals[rows, :] * gains[rows, :], axis=1, keepdims=True)
                obuf[rows, :] = (acc[rows, :] / total).astype(jnp.bfloat16)

            def send_back(there, _):
                piece = q_block * 8 + there
                source = obuf.at[pl.ds(pl.multiple_of(piece * PIECE, PIECE), PIECE), :]
                target = out_ref.at[:, pl.ds(pl.multiple_of(me * HEAD_DIM, HEAD_DIM), HEAD_DIM)]
                mine = (q_block == zh) & (there == x * 2 + zl)

                @pl.when(jnp.logical_not(mine))
                def _():
                    pltpu.make_async_remote_copy(
                        src_ref=source, dst_ref=target, send_sem=o_send, recv_sem=o_recv,
                        device_id=(there, y * 8 + q_block * 2 + core), device_id_type=MESH,
                    ).start()

                @pl.when(mine)
                def _():
                    pltpu.make_async_copy(source, target, self_sem.at[3]).start()

                return 0

            lax.fori_loop(0, 8, send_back, 0)
            return 0

        lax.fori_loop(0, 4, finish, 0)

        gone = kv.at[0, pl.ds(0, 3)]
        pltpu.make_async_copy(gone, gone, y_send).wait()
        pltpu.make_async_copy(kv.at[0], kv.at[0], sib_send).wait()
        others = out_ref.at[:, pl.ds(0, (HEADS - 1) * HEAD_DIM)]
        for n in range(3):
            pltpu.make_async_copy(others, others, in_send.at[n]).wait()
        sent = obuf.at[pl.ds(0, HALF - PIECE), :]
        with jax.named_scope("output sent"):
            pltpu.make_async_copy(sent, sent, o_send).wait()
        one = out_ref.at[:, pl.ds(0, HEAD_DIM)]
        pltpu.make_async_copy(one, one, self_sem.at[3]).wait()
        with jax.named_scope("output here"):
            pltpu.make_async_copy(others, others, o_recv).wait()

    @pl.when(jnp.logical_not(busy))
    def _():
        mask_copy.wait()
        for n in range(3):
            pltpu.make_async_copy(out_ref, out_ref, in_send.at[n]).wait()
        pltpu.make_async_copy(out_ref, out_ref, o_recv).wait()


def local(queries, key_rows, values, tile_mask):
    bf16, f32, dma = jnp.bfloat16, jnp.float32, pltpu.SemaphoreType.DMA
    queries, key_rows, values, tile_mask = (
        pltpu.with_memory_space_constraint(a, pltpu.HBM) for a in (queries, key_rows, values, tile_mask)
    )
    gathered = pl.pallas_call(
        kernel,
        out_shape=jax.ShapeDtypeStruct(queries.shape, bf16),
        in_specs=[pl.BlockSpec(memory_space=pltpu.HBM)] * 4,
        out_specs=pl.BlockSpec(memory_space=pltpu.VMEM),
        scratch_shapes=[
            pltpu.VMEM(tile_mask.shape, jnp.int32),
            pltpu.VMEM((3, *queries.shape), bf16),
            pltpu.VMEM((HALF, 2 * HEAD_DIM), bf16),
            pltpu.VMEM((2, LEVELS, 2, HALF, HEAD_DIM), bf16),
            pltpu.VMEM((8, HALF, HALF), bf16),
            pltpu.VMEM((HALF, TILE), f32),
            pltpu.VMEM((HALF, TILE), f32),
            pltpu.VMEM((HALF, TILE), f32),
            pltpu.VMEM((HALF, HEAD_DIM), f32),
            pltpu.VMEM((HALF, HEAD_DIM), bf16),
            dma((3, 4)),
            dma((3,)),
            dma((4,)),
            dma((2, 3, 4)),
            dma,
            dma((2, 4)),
            dma,
            dma,
            dma,
            dma,
            dma((3,)),
        ],
        compiler_params=pltpu.CompilerParams(
            collective_id=0, has_side_effects=True, vmem_limit_bytes=48 * 2**20
        ),
    )(queries, key_rows, values, tile_mask)
    return gathered.astype(f32)


def solution(mesh):
    return jax.shard_map(
        local,
        mesh=mesh,
        in_specs=(
            P(("blk", "head"), None),
            P(("blk", "head"), None),
            P(("blk", "head"), None),
            P(),
        ),
        out_specs=P(("blk", "head"), None),
        check_vma=False,
    )
```

```python
import jax
import jax.numpy as jnp
from jax import lax
from jax.experimental import pallas as pl
from jax.experimental.pallas import tpu as pltpu
from jax.sharding import PartitionSpec as P

MESH = pl.DeviceIdType.MESH

HEADS = 24
HEAD_DIM = 128
TILE = 128
PIECE = 32
LEVELS = 4
HALF = 1024
SLAB = 256
ORDER = (0, 1, 3, 2)
GOES_UP = (0, 3)
MASKED = -1e30
SCALE2 = HEAD_DIM**-0.5 * 1.4426950408889634


def place():
    head, blk = lax.axis_index("head"), lax.axis_index("blk")
    return head // 2, blk // 8, (blk // 2) % 4, head % 2, blk % 2


def column_of(head):
    return head // 8, head % 8


def device_at(x, y, z, core):
    return (x * 2 + z % 2, y * 8 + (z // 2) * 2 + core)


def span(r):
    return max(0, r - 2) * SLAB, (min(3, r + 2) + 1) * SLAB


def kernel(
    q_ref, k_ref, v_ref, mask_ref, out_ref,
    mask, rows_in, qa, kv, wbuf, peaks, totals, gains, acc, obuf,
    in_sem, in_send, self_sem, y_recv, y_send, sib_recv, sib_send, o_recv, o_send, mask_sem, load_sem,
):
    x, y, zh, zl, core = place()
    z = zh * 2 + zl
    me = x * 8 + z
    busy = x < 3
    slot = (zh * 8 + x * 2 + zl) * PIECE
    up, down, far = (y + 1) % 4, (y + 3) % 4, (y + 2) % 4
    levels = (y, down, up, far)
    sources = (rows_in.at[0], rows_in.at[1], rows_in.at[2])
    barrier = pltpu.get_barrier_semaphore()

    def greet(i, _):
        turn = i // 4
        far_off = (turn + 1) // 2
        hz = jnp.where(turn % 2 == 1, z + 4 - far_off, z + 4 + far_off) % 8
        hx = (x + 2 + i) % 4

        @pl.when((hx * 8 + hz != me) & (busy | (hx < 3)))
        def _():
            pl.semaphore_signal(
                barrier, inc=1, device_id=device_at(hx, y, hz, core), device_id_type=MESH
            )

        return 0

    lax.fori_loop(0, 32, greet, 0)

    @pl.when(busy)
    def _():
        for there in (
            device_at(x, up, z, core), device_at(x, down, z, core), device_at(x, y, z, 1 - core),
        ):
            pl.semaphore_signal(barrier, inc=1, device_id=there, device_id_type=MESH)

    loads = [
        pltpu.make_async_copy(ref, rows_in.at[n], load_sem.at[n])
        for n, ref in enumerate((k_ref, v_ref, q_ref))
    ]
    for n in (0, 2, 1):
        loads[n].start()

    mask_copy = pltpu.make_async_copy(mask_ref, mask, mask_sem)
    mask_copy.start()
    @pl.when(busy)
    def _():
        mask_copy.wait()
        for t in range(8):
            q_tile = y * 16 + (t // 2) * 4 + core * 2 + t % 2
            allowed = mask[pl.ds(q_tile, 1), :]
            bias = jnp.where(allowed > 0, 0.0, MASKED)
            bias = jnp.concatenate([bias, jnp.zeros_like(bias)], axis=1)
            qa[pl.ds(t * TILE, TILE), pl.ds(HEAD_DIM, TILE)] = jnp.broadcast_to(
                bias, (TILE, TILE)
            ).astype(jnp.bfloat16)
        peaks[...] = jnp.full(peaks.shape, MASKED, jnp.float32)
        totals[...] = jnp.zeros(totals.shape, jnp.float32)
        acc[...] = jnp.zeros(acc.shape, jnp.float32)

        wbuf[7, pl.ds(0, SLAB), pl.ds(3 * SLAB, SLAB)] = jnp.zeros((SLAB, SLAB), jnp.bfloat16)
        wbuf[7, pl.ds(3 * SLAB, SLAB), pl.ds(0, SLAB)] = jnp.zeros((SLAB, SLAB), jnp.bfloat16)

    with jax.named_scope("barrier"):
        @pl.when(busy)
        def _():
            pl.semaphore_wait(barrier, 34)

        @pl.when(jnp.logical_not(busy))
        def _():
            pl.semaphore_wait(barrier, HEADS)


    def landing(n):
        if n == 2:
            return qa.at[pl.ds(slot, PIECE), pl.ds(0, HEAD_DIM)]
        return kv.at[n, y, core, pl.ds(slot, PIECE), :]

    def slab_rows(rel):
        return pl.ds(pl.multiple_of((zh + rel) % 4 * SLAB, SLAB), SLAB)

    def send_pieces(n):
        def send_piece(i, _):
            turn, w = i // 6, i % 6
            off = jnp.where(turn < 2, turn, 5 - turn)
            hz = (zh + off) % 4 * 2 + w % 2
            hx = (x + w // 2) % 3
            head = hx * 8 + hz
            source = sources[n].at[:, pl.ds(pl.multiple_of(head * HEAD_DIM, HEAD_DIM), HEAD_DIM)]

            @pl.when(head != me)
            def _():
                pltpu.make_async_remote_copy(
                    src_ref=source, dst_ref=landing(n), send_sem=in_send.at[n],
                    recv_sem=in_sem.at[n, (4 - off) % 4],
                    device_id=device_at(hx, y, hz, core), device_id_type=MESH,
                ).start()

            @pl.when(head == me)
            def _():
                pltpu.make_async_copy(source, landing(n), self_sem.at[n]).start()

            return 0

        lax.fori_loop(0, HEADS, send_piece, 0)

    with jax.named_scope("pieces out"):
        for n in (0, 2, 1):
            loads[n].wait()
            send_pieces(n)

    def wait_slab(n, rel):
        if rel == 0:
            part = kv.at[0, 0, 0, pl.ds(0, SLAB - PIECE), :]
            pltpu.make_async_copy(part, part, in_sem.at[n, 0]).wait()
            pltpu.make_async_copy(landing(n), landing(n), self_sem.at[n]).wait()
        else:
            part = kv.at[0, 0, 0, pl.ds(0, SLAB), :]
            pltpu.make_async_copy(part, part, in_sem.at[n, rel]).wait()

    def y_copy(n, level, rel, way):
        part = kv.at[n, level, core, slab_rows(rel), :]
        upward = rel in GOES_UP if way == 2 else way == 0
        return pltpu.make_async_remote_copy(
            src_ref=part, dst_ref=part, send_sem=y_send, recv_sem=y_recv.at[n, way, rel],
            device_id=device_at(x, up if upward else down, z, core), device_id_type=MESH,
        )

    def to_sibling(n, step, rel=None):
        part = kv.at[n, levels[step], core]
        if rel is not None:
            part = part.at[slab_rows(rel), :]
        pltpu.make_async_remote_copy(
            src_ref=part, dst_ref=part, send_sem=sib_send, recv_sem=sib_recv.at[n, step],
            device_id=device_at(x, y, z, 1 - core), device_id_type=MESH,
        ).start()

    def own_slab(n, rel):
        wait_slab(n, rel)
        y_copy(n, y, rel, 0).start()
        y_copy(n, y, rel, 1).start()
        if rel == ORDER[-1]:
            to_sibling(n, 0)

    def next_slab(n, rel):
        y_copy(n, down, rel, 0).wait_recv()
        if rel in GOES_UP:
            y_copy(n, down, rel, 2).start()
        y_copy(n, up, rel, 1).wait_recv()
        if rel not in GOES_UP:
            y_copy(n, up, rel, 2).start()
        if rel == ORDER[-1]:
            to_sibling(n, 1)
            to_sibling(n, 2)

    def far_slab(n, rel):
        y_copy(n, far, rel, 2).wait_recv()
        if n == 1:
            to_sibling(n, 3, rel)
        elif rel == ORDER[-1]:
            to_sibling(n, 3)

    def from_sibling(n, step):
        part = kv.at[n, levels[step], 1 - core]
        pltpu.make_async_copy(part, part, sib_recv.at[n, step]).wait()

    def turn(i):
        step = i // 2
        off = jnp.where(step == 0, 0, jnp.where(step == 1, 3, jnp.where(step == 2, 1, 2)))
        return (y + off) % 4, (core + i) % 2

    def weigh(i, block=None):
        level, whose = turn(i)
        for r in range(4):
            lo, hi = span(r)
            rows = pl.ds(lo, hi - lo) if block is None else block
            lane = lax.broadcasted_iota(jnp.int32, (SLAB, TILE), 1)
            row = lax.broadcasted_iota(jnp.int32, (SLAB, TILE), 0)
            hot = lane == level * 16 + r * 4 + whose * 2 + row // TILE
            keys = jnp.concatenate(
                [
                    kv[0, level, whose, r * SLAB : (r + 1) * SLAB, :],
                    jnp.where(hot, 1.0, 0.0).astype(jnp.bfloat16),
                ],
                axis=1,
            )
            scores = lax.dot_general(
                qa[rows, :], keys, (((1,), (1,)), ((), ())), preferred_element_type=jnp.float32
            )
            peak = jnp.max(scores, axis=1, keepdims=True)
            weights = jnp.exp2((scores - peak) * SCALE2)
            wbuf[i, rows, r * SLAB : (r + 1) * SLAB] = weights.astype(jnp.bfloat16)
            before = peaks[rows, :]
            here = lax.broadcasted_iota(jnp.int32, before.shape, 1) == i * 4 + r
            peaks[rows, :] = jnp.where(here, peak, before)

    def mix(i, block=None):
        level, whose = turn(i)
        for r in range(4):
            lo, hi = span(r)
            rows = pl.ds(lo, hi - lo) if block is None else block
            lane = lax.broadcasted_iota(jnp.int32, (SLAB, TILE), 1)
            vals = jnp.concatenate(
                [
                    kv[1, level, whose, r * SLAB : (r + 1) * SLAB, :],
                    jnp.where(lane == i * 4 + r, 1.0, 0.0).astype(jnp.bfloat16),
                ],
                axis=1,
            )
            mixed = jnp.dot(
                wbuf[i, rows, r * SLAB : (r + 1) * SLAB], vals, preferred_element_type=jnp.float32
            )
            gain = gains[rows, :]
            here = lax.broadcasted_iota(jnp.int32, gain.shape, 1) == i * 4 + r
            gain = jnp.sum(jnp.where(here, gain, 0.0), axis=1, keepdims=True)
            acc[rows, :] += mixed[:, :HEAD_DIM] * gain
            totals[rows, :] += mixed[:, HEAD_DIM:]

    def near(i):
        level, _ = turn(i)
        return jnp.abs(level - y) < 3

    @pl.when(busy)
    def _():
        own_slab(0, 0)
        own_slab(0, 1)
        own_slab(0, 3)
        own_slab(0, 2)
        next_slab(0, 0)
        next_slab(0, 1)

        def run_hooks(hooks, i):
            if isinstance(i, int):
                for call, n, which in hooks.get(i, ()):
                    call(n, which)
                return
            for at, calls in hooks.items():

                @pl.when(i == at)
                def _(calls=calls):
                    for call, n, which in calls:
                        call(n, which)

        def weigh_own(pair, turns):
            with jax.named_scope("weigh own"):
                for i in turns:
                    for rel in pair:
                        weigh(i, slab_rows(rel))

        wait_slab(2, 0)
        wait_slab(2, 1)
        weigh_own((0, 1), (0,))
        next_slab(0, 3)
        from_sibling(0, 0)
        weigh_own((0, 1), (1,))
        next_slab(0, 2)
        wait_slab(2, 3)
        wait_slab(2, 2)
        own_slab(1, 0)
        weigh_own((3, 2), (0, 1))

        weigh_hooks = {
            2: ((own_slab, 1, 1),),
            3: ((own_slab, 1, 3), (from_sibling, 0, 1)),
            4: ((own_slab, 1, 2), (far_slab, 0, 0), (far_slab, 0, 1), (far_slab, 0, 3), (far_slab, 0, 2)),
            5: ((from_sibling, 0, 2),),
            6: ((next_slab, 1, 0),),
            7: ((next_slab, 1, 1), (from_sibling, 0, 3)),
        }
        mix_hooks = {
            0: ((next_slab, 1, 3), (next_slab, 1, 2), (from_sibling, 1, 0)),
            3: ((far_slab, 1, 0),),
            4: ((far_slab, 1, 1), (from_sibling, 1, 1)),
            5: ((from_sibling, 1, 2), (far_slab, 1, 3), (far_slab, 1, 2)),
        }

        def weigh_turn(i, _):
            run_hooks(weigh_hooks, i)

            def _():
                with jax.named_scope("weigh"):
                    weigh(i)

            _() if i > 5 else pl.when(near(i))(_)

            return 0

        for i in range(2, 8):
            weigh_turn(i, 0)
        every = peaks[...]
        gains[...] = jnp.exp2((every - jnp.max(every, axis=1, keepdims=True)) * SCALE2)

        def mix_turn(m, _):
            run_hooks(mix_hooks, m)
            i = (0, 1, 2, 4, 3, 5, 6)[m]

            def _():
                with jax.named_scope("mix"):
                    mix(i)

            _() if i > 5 or i < 2 else pl.when(near(i))(_)

            return 0

        run_hooks(mix_hooks, 0)
        with jax.named_scope("mix"):
            mix(0)
            mix(1)
        for m in range(2, 7):
            mix_turn(m, 0)
        from_sibling(1, 3)

        def finish(q_block, _):
            rows = pl.ds(pl.multiple_of(q_block * SLAB, SLAB), SLAB)
            with jax.named_scope("last mix"):
                mix(7, rows)
                total = jnp.sum(totals[rows, :] * gains[rows, :], axis=1, keepdims=True)
                obuf[rows, :] = (acc[rows, :] / total).astype(jnp.bfloat16)

            def send_back(i, _):
                there = (i + x * 2 + zl) % 8
                piece = q_block * 8 + there
                source = obuf.at[pl.ds(pl.multiple_of(piece * PIECE, PIECE), PIECE), :]
                target = out_ref.at[:, pl.ds(pl.multiple_of(me * HEAD_DIM, HEAD_DIM), HEAD_DIM)]
                mine = (q_block == zh) & (there == x * 2 + zl)

                @pl.when(jnp.logical_not(mine))
                def _():
                    pltpu.make_async_remote_copy(
                        src_ref=source, dst_ref=target, send_sem=o_send, recv_sem=o_recv,
                        device_id=(there, y * 8 + q_block * 2 + core), device_id_type=MESH,
                    ).start()

                @pl.when(mine)
                def _():
                    pltpu.make_async_copy(source, target, self_sem.at[3]).start()

                return 0

            lax.fori_loop(0, 8, send_back, 0)
            return 0

        lax.fori_loop(0, 4, finish, 0)

        gone = kv.at[0, pl.ds(0, 3)]
        pltpu.make_async_copy(gone, gone, y_send).wait()
        pltpu.make_async_copy(kv.at[0], kv.at[0], sib_send).wait()
        others = out_ref.at[:, pl.ds(0, (HEADS - 1) * HEAD_DIM)]
        for n in range(3):
            pltpu.make_async_copy(others, others, in_send.at[n]).wait()
        sent = obuf.at[pl.ds(0, HALF - PIECE), :]
        with jax.named_scope("output sent"):
            pltpu.make_async_copy(sent, sent, o_send).wait()
        one = out_ref.at[:, pl.ds(0, HEAD_DIM)]
        pltpu.make_async_copy(one, one, self_sem.at[3]).wait()
        with jax.named_scope("output here"):
            pltpu.make_async_copy(others, others, o_recv).wait()

    @pl.when(jnp.logical_not(busy))
    def _():
        mask_copy.wait()
        for n in range(3):
            pltpu.make_async_copy(out_ref, out_ref, in_send.at[n]).wait()
        pltpu.make_async_copy(out_ref, out_ref, o_recv).wait()


def local(queries, key_rows, values, tile_mask):
    bf16, f32, dma = jnp.bfloat16, jnp.float32, pltpu.SemaphoreType.DMA
    queries, key_rows, values, tile_mask = (
        pltpu.with_memory_space_constraint(a, pltpu.HBM) for a in (queries, key_rows, values, tile_mask)
    )
    gathered = pl.pallas_call(
        kernel,
        out_shape=jax.ShapeDtypeStruct(queries.shape, bf16),
        in_specs=[pl.BlockSpec(memory_space=pltpu.HBM)] * 4,
        out_specs=pl.BlockSpec(memory_space=pltpu.VMEM),
        scratch_shapes=[
            pltpu.VMEM(tile_mask.shape, jnp.int32),
            pltpu.VMEM((3, *queries.shape), bf16),
            pltpu.VMEM((HALF, 2 * HEAD_DIM), bf16),
            pltpu.VMEM((2, LEVELS, 2, HALF, HEAD_DIM), bf16),
            pltpu.VMEM((8, HALF, HALF), bf16),
            pltpu.VMEM((HALF, TILE), f32),
            pltpu.VMEM((HALF, TILE), f32),
            pltpu.VMEM((HALF, TILE), f32),
            pltpu.VMEM((HALF, HEAD_DIM), f32),
            pltpu.VMEM((HALF, HEAD_DIM), bf16),
            dma((3, 4)),
            dma((3,)),
            dma((4,)),
            dma((2, 3, 4)),
            dma,
            dma((2, 4)),
            dma,
            dma,
            dma,
            dma,
            dma((3,)),
        ],
        compiler_params=pltpu.CompilerParams(
            collective_id=0, has_side_effects=True, vmem_limit_bytes=48 * 2**20
        ),
    )(queries, key_rows, values, tile_mask)
    return gathered.astype(f32)


def solution(mesh):
    return jax.shard_map(
        local,
        mesh=mesh,
        in_specs=(
            P(("blk", "head"), None),
            P(("blk", "head"), None),
            P(("blk", "head"), None),
            P(),
        ),
        out_specs=P(("blk", "head"), None),
        check_vma=False,
    )
```

```python
import jax
import jax.numpy as jnp
from jax import lax
from jax.experimental import pallas as pl
from jax.experimental.pallas import tpu as pltpu
from jax.sharding import PartitionSpec as P

MESH = pl.DeviceIdType.MESH

HEADS = 24
HEAD_DIM = 128
TILE = 128
PIECE = 32
LEVELS = 4
HALF = 1024
SLAB = 256
ORDER = (0, 1, 3, 2)
GOES_UP = (0, 3)
MASKED = -1e30
SCALE2 = HEAD_DIM**-0.5 * 1.4426950408889634


def place():
    head, blk = lax.axis_index("head"), lax.axis_index("blk")
    return head // 2, blk // 8, (blk // 2) % 4, head % 2, blk % 2


def column_of(head):
    return head // 8, head % 8


def device_at(x, y, z, core):
    return (x * 2 + z % 2, y * 8 + (z // 2) * 2 + core)


def span(r):
    return max(0, r - 2) * SLAB, (min(3, r + 2) + 1) * SLAB


def kernel(
    q_ref, k_ref, v_ref, mask_ref, out_ref,
    mask, rows_in, qa, kv, wbuf, peaks, totals, gains, acc, obuf,
    in_sem, in_send, self_sem, y_recv, y_send, sib_recv, sib_send, o_recv, o_send, mask_sem, load_sem,
):
    x, y, zh, zl, core = place()
    z = zh * 2 + zl
    me = x * 8 + z
    busy = x < 3
    slot = (zh * 8 + x * 2 + zl) * PIECE
    up, down, far = (y + 1) % 4, (y + 3) % 4, (y + 2) % 4
    levels = (y, down, up, far)
    sources = (rows_in.at[0], rows_in.at[1], rows_in.at[2])
    barrier = pltpu.get_barrier_semaphore()

    def greet(i, _):
        turn = i // 4
        far_off = (turn + 1) // 2
        hz = jnp.where(turn % 2 == 1, z + 4 - far_off, z + 4 + far_off) % 8
        hx = (x + 2 + i) % 4

        @pl.when((hx * 8 + hz != me) & (busy | (hx < 3)))
        def _():
            pl.semaphore_signal(
                barrier, inc=1, device_id=device_at(hx, y, hz, core), device_id_type=MESH
            )

        return 0

    lax.fori_loop(0, 32, greet, 0)

    @pl.when(busy)
    def _():
        for there in (
            device_at(x, up, z, core), device_at(x, down, z, core), device_at(x, y, z, 1 - core),
        ):
            pl.semaphore_signal(barrier, inc=1, device_id=there, device_id_type=MESH)

    loads = [
        pltpu.make_async_copy(ref, rows_in.at[n], load_sem.at[n])
        for n, ref in enumerate((k_ref, v_ref, q_ref))
    ]
    for n in (0, 2, 1):
        loads[n].start()

    mask_copy = pltpu.make_async_copy(mask_ref, mask, mask_sem)
    mask_copy.start()
    @pl.when(busy)
    def _():
        mask_copy.wait()
        for t in range(8):
            q_tile = y * 16 + (t // 2) * 4 + core * 2 + t % 2
            allowed = mask[pl.ds(q_tile, 1), :]
            bias = jnp.where(allowed > 0, 0.0, MASKED)
            bias = jnp.concatenate([bias, jnp.zeros_like(bias)], axis=1)
            qa[pl.ds(t * TILE, TILE), pl.ds(HEAD_DIM, TILE)] = jnp.broadcast_to(
                bias, (TILE, TILE)
            ).astype(jnp.bfloat16)
        peaks[...] = jnp.full(peaks.shape, MASKED, jnp.float32)
        totals[...] = jnp.zeros(totals.shape, jnp.float32)
        acc[...] = jnp.zeros(acc.shape, jnp.float32)

        wbuf[7, pl.ds(0, SLAB), pl.ds(3 * SLAB, SLAB)] = jnp.zeros((SLAB, SLAB), jnp.bfloat16)
        wbuf[7, pl.ds(3 * SLAB, SLAB), pl.ds(0, SLAB)] = jnp.zeros((SLAB, SLAB), jnp.bfloat16)

    with jax.named_scope("barrier"):
        @pl.when(busy)
        def _():
            pl.semaphore_wait(barrier, 34)

        @pl.when(jnp.logical_not(busy))
        def _():
            pl.semaphore_wait(barrier, HEADS)


    def landing(n):
        if n == 2:
            return qa.at[pl.ds(slot, PIECE), pl.ds(0, HEAD_DIM)]
        return kv.at[n, y, core, pl.ds(slot, PIECE), :]

    def slab_rows(rel):
        return pl.ds(pl.multiple_of((zh + rel) % 4 * SLAB, SLAB), SLAB)

    def send_pieces(n):
        def send_piece(i, _):
            turn, w = i // 6, i % 6
            off = jnp.where(turn < 2, turn, 5 - turn)
            hz = (zh + off) % 4 * 2 + w % 2
            hx = (x + w // 2) % 3
            head = hx * 8 + hz
            source = sources[n].at[:, pl.ds(pl.multiple_of(head * HEAD_DIM, HEAD_DIM), HEAD_DIM)]

            @pl.when(head != me)
            def _():
                pltpu.make_async_remote_copy(
                    src_ref=source, dst_ref=landing(n), send_sem=in_send.at[n],
                    recv_sem=in_sem.at[n, (4 - off) % 4],
                    device_id=device_at(hx, y, hz, core), device_id_type=MESH,
                ).start()

            @pl.when(head == me)
            def _():
                pltpu.make_async_copy(source, landing(n), self_sem.at[n]).start()

            return 0

        lax.fori_loop(0, HEADS, send_piece, 0)

    with jax.named_scope("pieces out"):
        for n in (0, 2, 1):
            loads[n].wait()
            send_pieces(n)

    def wait_slab(n, rel):
        if rel == 0:
            part = kv.at[0, 0, 0, pl.ds(0, SLAB - PIECE), :]
            pltpu.make_async_copy(part, part, in_sem.at[n, 0]).wait()
            pltpu.make_async_copy(landing(n), landing(n), self_sem.at[n]).wait()
        else:
            part = kv.at[0, 0, 0, pl.ds(0, SLAB), :]
            pltpu.make_async_copy(part, part, in_sem.at[n, rel]).wait()

    def y_copy(n, level, rel, way):
        part = kv.at[n, level, core, slab_rows(rel), :]
        upward = rel in GOES_UP if way == 2 else way == 0
        return pltpu.make_async_remote_copy(
            src_ref=part, dst_ref=part, send_sem=y_send, recv_sem=y_recv.at[n, way, rel],
            device_id=device_at(x, up if upward else down, z, core), device_id_type=MESH,
        )

    def to_sibling(n, step, rel=None):
        part = kv.at[n, levels[step], core]
        if rel is not None:
            part = part.at[slab_rows(rel), :]
        pltpu.make_async_remote_copy(
            src_ref=part, dst_ref=part, send_sem=sib_send, recv_sem=sib_recv.at[n, step],
            device_id=device_at(x, y, z, 1 - core), device_id_type=MESH,
        ).start()

    def own_slab(n, rel):
        wait_slab(n, rel)
        y_copy(n, y, rel, 0).start()
        y_copy(n, y, rel, 1).start()
        if rel == ORDER[-1]:
            to_sibling(n, 0)

    def next_slab(n, rel):
        y_copy(n, down, rel, 0).wait_recv()
        if rel in GOES_UP:
            y_copy(n, down, rel, 2).start()
        y_copy(n, up, rel, 1).wait_recv()
        if rel not in GOES_UP:
            y_copy(n, up, rel, 2).start()
        if rel == ORDER[-1]:
            to_sibling(n, 1)
            to_sibling(n, 2)

    def far_slab(n, rel):
        y_copy(n, far, rel, 2).wait_recv()
        if n == 1:
            to_sibling(n, 3, rel)
        elif rel == ORDER[-1]:
            to_sibling(n, 3)

    def from_sibling(n, step):
        part = kv.at[n, levels[step], 1 - core]
        pltpu.make_async_copy(part, part, sib_recv.at[n, step]).wait()

    def turn(i):
        step = i // 2
        off = jnp.where(step == 0, 0, jnp.where(step == 1, 3, jnp.where(step == 2, 1, 2)))
        return (y + off) % 4, (core + i) % 2

    def weigh(i, block=None):
        level, whose = turn(i)
        for r in range(4):
            lo, hi = span(r)
            rows = pl.ds(lo, hi - lo) if block is None else block
            lane = lax.broadcasted_iota(jnp.int32, (SLAB, TILE), 1)
            row = lax.broadcasted_iota(jnp.int32, (SLAB, TILE), 0)
            hot = lane == level * 16 + r * 4 + whose * 2 + row // TILE
            keys = jnp.concatenate(
                [
                    kv[0, level, whose, r * SLAB : (r + 1) * SLAB, :],
                    jnp.where(hot, 1.0, 0.0).astype(jnp.bfloat16),
                ],
                axis=1,
            )
            scores = lax.dot_general(
                qa[rows, :], keys, (((1,), (1,)), ((), ())), preferred_element_type=jnp.float32
            )
            peak = jnp.max(scores, axis=1, keepdims=True)
            weights = jnp.exp2((scores - peak) * SCALE2)
            wbuf[i, rows, r * SLAB : (r + 1) * SLAB] = weights.astype(jnp.bfloat16)
            before = peaks[rows, :]
            here = lax.broadcasted_iota(jnp.int32, before.shape, 1) == i * 4 + r
            peaks[rows, :] = jnp.where(here, peak, before)

    def mix(i, block=None):
        level, whose = turn(i)
        for r in range(4):
            lo, hi = span(r)
            rows = pl.ds(lo, hi - lo) if block is None else block
            lane = lax.broadcasted_iota(jnp.int32, (SLAB, TILE), 1)
            vals = jnp.concatenate(
                [
                    kv[1, level, whose, r * SLAB : (r + 1) * SLAB, :],
                    jnp.where(lane == i * 4 + r, 1.0, 0.0).astype(jnp.bfloat16),
                ],
                axis=1,
            )
            mixed = jnp.dot(
                wbuf[i, rows, r * SLAB : (r + 1) * SLAB], vals, preferred_element_type=jnp.float32
            )
            gain = gains[rows, :]
            here = lax.broadcasted_iota(jnp.int32, gain.shape, 1) == i * 4 + r
            gain = jnp.sum(jnp.where(here, gain, 0.0), axis=1, keepdims=True)
            acc[rows, :] += mixed[:, :HEAD_DIM] * gain
            totals[rows, :] += mixed[:, HEAD_DIM:]

    def near(i):
        level, _ = turn(i)
        return jnp.abs(level - y) < 3

    @pl.when(busy)
    def _():
        own_slab(0, 0)
        own_slab(0, 1)
        own_slab(0, 3)
        own_slab(0, 2)
        next_slab(0, 0)
        next_slab(0, 1)

        def run_hooks(hooks, i):
            if isinstance(i, int):
                for call, n, which in hooks.get(i, ()):
                    call(n, which)
                return
            for at, calls in hooks.items():

                @pl.when(i == at)
                def _(calls=calls):
                    for call, n, which in calls:
                        call(n, which)

        own_hooks = {
            0: ((wait_slab, 2, 0), (wait_slab, 2, 1)),
            1: ((next_slab, 0, 3), (from_sibling, 0, 0)),
            2: ((next_slab, 0, 2), (wait_slab, 2, 3), (wait_slab, 2, 2)),
            3: ((own_slab, 1, 0),),
        }

        def weigh_own(j, _):
            run_hooks(own_hooks, j)
            with jax.named_scope("weigh own"):
                for k in range(2):
                    weigh(j % 2, slab_rows(jnp.where(j < 2, k, 3 - k)))
            return 0

        lax.fori_loop(0, 4, weigh_own, 0)

        weigh_hooks = {
            2: ((own_slab, 1, 1),),
            3: ((own_slab, 1, 3), (from_sibling, 0, 1)),
            4: ((own_slab, 1, 2), (far_slab, 0, 0), (far_slab, 0, 1), (far_slab, 0, 3), (far_slab, 0, 2)),
            5: ((from_sibling, 0, 2),),
            6: ((next_slab, 1, 0),),
            7: ((next_slab, 1, 1), (from_sibling, 0, 3)),
        }
        mix_hooks = {
            0: ((next_slab, 1, 3),),
            1: ((next_slab, 1, 2), (from_sibling, 1, 0)),
            3: ((far_slab, 1, 0),),
            4: ((far_slab, 1, 1), (from_sibling, 1, 1)),
            5: ((from_sibling, 1, 2), (far_slab, 1, 3)),
            6: ((far_slab, 1, 2),),
        }

        def weigh_turn(i, _):
            run_hooks(weigh_hooks, i)

            def _():
                with jax.named_scope("weigh"):
                    weigh(i)

            _() if i > 5 else pl.when(near(i))(_)

            return 0

        for i in range(2, 8):
            weigh_turn(i, 0)
        every = peaks[...]
        gains[...] = jnp.exp2((every - jnp.max(every, axis=1, keepdims=True)) * SCALE2)

        def mix_turn(m, _):
            run_hooks(mix_hooks, m)
            i = (0, 1, 2, 4, 3, 5, 6)[m]

            def _():
                with jax.named_scope("mix"):
                    mix(i)

            _() if i > 5 or i < 2 else pl.when(near(i))(_)

            return 0

        for m in range(7):
            mix_turn(m, 0)
        from_sibling(1, 3)

        def finish(q_block, _):
            rows = pl.ds(pl.multiple_of(q_block * SLAB, SLAB), SLAB)
            with jax.named_scope("last mix"):
                mix(7, rows)
                total = jnp.sum(totals[rows, :] * gains[rows, :], axis=1, keepdims=True)
                obuf[rows, :] = (acc[rows, :] / total).astype(jnp.bfloat16)

            def send_back(i, _):
                there = (i + x * 2 + zl) % 8
                piece = q_block * 8 + there
                source = obuf.at[pl.ds(pl.multiple_of(piece * PIECE, PIECE), PIECE), :]
                target = out_ref.at[:, pl.ds(pl.multiple_of(me * HEAD_DIM, HEAD_DIM), HEAD_DIM)]
                mine = (q_block == zh) & (there == x * 2 + zl)

                @pl.when(jnp.logical_not(mine))
                def _():
                    pltpu.make_async_remote_copy(
                        src_ref=source, dst_ref=target, send_sem=o_send, recv_sem=o_recv,
                        device_id=(there, y * 8 + q_block * 2 + core), device_id_type=MESH,
                    ).start()

                @pl.when(mine)
                def _():
                    pltpu.make_async_copy(source, target, self_sem.at[3]).start()

                return 0

            lax.fori_loop(0, 8, send_back, 0)
            return 0

        lax.fori_loop(0, 4, finish, 0)

        gone = kv.at[0, pl.ds(0, 3)]
        pltpu.make_async_copy(gone, gone, y_send).wait()
        pltpu.make_async_copy(kv.at[0], kv.at[0], sib_send).wait()
        others = out_ref.at[:, pl.ds(0, (HEADS - 1) * HEAD_DIM)]
        for n in range(3):
            pltpu.make_async_copy(others, others, in_send.at[n]).wait()
        sent = obuf.at[pl.ds(0, HALF - PIECE), :]
        with jax.named_scope("output sent"):
            pltpu.make_async_copy(sent, sent, o_send).wait()
        one = out_ref.at[:, pl.ds(0, HEAD_DIM)]
        pltpu.make_async_copy(one, one, self_sem.at[3]).wait()
        with jax.named_scope("output here"):
            pltpu.make_async_copy(others, others, o_recv).wait()

    @pl.when(jnp.logical_not(busy))
    def _():
        mask_copy.wait()
        for n in range(3):
            pltpu.make_async_copy(out_ref, out_ref, in_send.at[n]).wait()
        pltpu.make_async_copy(out_ref, out_ref, o_recv).wait()


def local(queries, key_rows, values, tile_mask):
    bf16, f32, dma = jnp.bfloat16, jnp.float32, pltpu.SemaphoreType.DMA
    queries, key_rows, values, tile_mask = (
        pltpu.with_memory_space_constraint(a, pltpu.HBM) for a in (queries, key_rows, values, tile_mask)
    )
    gathered = pl.pallas_call(
        kernel,
        out_shape=jax.ShapeDtypeStruct(queries.shape, bf16),
        in_specs=[pl.BlockSpec(memory_space=pltpu.HBM)] * 4,
        out_specs=pl.BlockSpec(memory_space=pltpu.VMEM),
        scratch_shapes=[
            pltpu.VMEM(tile_mask.shape, jnp.int32),
            pltpu.VMEM((3, *queries.shape), bf16),
            pltpu.VMEM((HALF, 2 * HEAD_DIM), bf16),
            pltpu.VMEM((2, LEVELS, 2, HALF, HEAD_DIM), bf16),
            pltpu.VMEM((8, HALF, HALF), bf16),
            pltpu.VMEM((HALF, TILE), f32),
            pltpu.VMEM((HALF, TILE), f32),
            pltpu.VMEM((HALF, TILE), f32),
            pltpu.VMEM((HALF, HEAD_DIM), f32),
            pltpu.VMEM((HALF, HEAD_DIM), bf16),
            dma((3, 4)),
            dma((3,)),
            dma((4,)),
            dma((2, 3, 4)),
            dma,
            dma((2, 4)),
            dma,
            dma,
            dma,
            dma,
            dma((3,)),
        ],
        compiler_params=pltpu.CompilerParams(
            collective_id=0, has_side_effects=True, vmem_limit_bytes=48 * 2**20
        ),
    )(queries, key_rows, values, tile_mask)
    return gathered.astype(f32)


def solution(mesh):
    return jax.shard_map(
        local,
        mesh=mesh,
        in_specs=(
            P(("blk", "head"), None),
            P(("blk", "head"), None),
            P(("blk", "head"), None),
            P(),
        ),
        out_specs=P(("blk", "head"), None),
        check_vma=False,
    )
```
